32 devices in a mesh: row: 4 (over z), col: 8 (over y, x, core).
Axes of the slice: x: 2, y: 2, z: 4, core: 2. Of those that a mesh axis runs over, the one named last changes fastest.
Arguments:
- tokens: bfloat16 [512, 12288], P('col', 'row'), may hold values from -6 to 6
- out_grad: bfloat16 [512, 49152], P('row', 'col'), may hold values from -6 to 6
- weight: bfloat16 [12288, 49152], P('row', 'col'), may hold values from -0.09375 to 0.09375
- block_mask: int32 [48, 192], P('row', 'col'), may hold values 0 or 1
Outputs:
- input_grad: bfloat16 [512, 12288], P('col', 'row')
- weight_grad: bfloat16 [12288, 49152], P('row', 'col')
The draws below stay inside these ranges and needn't reach their ends.
All inputs are finite; a program needn't handle non-finite values. No bound on the sum of `block_mask` on one device may be relied on, other than what follows from the above.
Results may differ from the reference program's by a relative error of at most 0.015.
Values may be sent and summed in bfloat16 or wider, within the bound.
No kernel may reach another device: no remote copies, remote signals or barrier semaphores. Data moves between devices by JAX's collectives and lax.ppermute only.
A program may use at most 320 MiB of HBM per device.

```python
import jax
import jax.numpy as jnp
from jax import lax

D = 12288
FF = 49152
BLOCK = 256
TOKENS = 512
N_COL = 8


def set_ends(array, key, low, top_value):
    spot = [jax.random.randint(jax.random.fold_in(key, axis), (), 0, length) for axis, length in enumerate(array.shape)]
    longest = array.shape.index(max(array.shape))
    neighbour = spot[:longest] + [(spot[longest] + 1) % array.shape[longest]] + spot[longest + 1:]
    return array.at[tuple(spot)].set(low).at[tuple(neighbour)].set(top_value)


def with_spikes(result, key, source, target, blocks, factor):
    def block_of(position):
        return (jnp.arange(result.shape[position]) // (result.shape[position] // blocks)).reshape((-1,) + (1,) * (result.ndim - 1 - position))

    first = jax.random.permutation(key, blocks)[block_of(target)]
    far = (block_of(target) + blocks // 2) % blocks
    return jnp.where((block_of(source) == first) | (block_of(source) == far), factor * result, result)


def level_of(rng, extent, split, low, largest):
    def one(dim, parts):
        heights = jax.random.uniform(jax.random.fold_in(jax.random.fold_in(rng, 6), dim), (parts,), jnp.float32, low / len(split), largest / len(split))
        return jnp.repeat(jnp.exp(heights), extent[dim] // parts).reshape((-1,) + (1,) * (len(extent) - dim - 1))

    gain = one(*split[0])
    for cut in split[1:]:
        gain = gain * one(*cut)
    return gain


def scatter_about(key, shape, deviation, bound, split=(), kind=jnp.bfloat16):
    result = jax.random.normal(key, shape, jnp.float32) * deviation
    if len(split) > 0:
        result = level_of(key, shape, split, -0.22, 0.18) * result
    return jnp.clip(result, min=-bound, max=bound).astype(kind)


def gaussian_with(stream_key, dims, spread, most, pieces, heavy, kind=jnp.bfloat16):
    values = spread * jax.random.normal(stream_key, dims, jnp.float32)
    if pieces:
        values = values * level_of(stream_key, dims, pieces, -0.22, 0.18)
    return jnp.clip(with_spikes(values, jax.random.fold_in(stream_key, 3), *heavy), -most, most).astype(kind)


def setup_inputs(seed: int = 0) -> dict:
    key_of = jax.random.split(jax.random.key(seed), 5)
    tokens = scatter_about(key_of[0], (TOKENS, D), 1.0, 6.0, ((0, 8), (1, 4)))
    out_grad = gaussian_with(key_of[1], (TOKENS, FF), 1.0, 6.0, ((0, 4), (1, 8)), (1, 0, 8, 2.0))
    weight = scatter_about(key_of[2], (D, FF), (3 * D // 10) ** -0.5, 0.09375, ((0, 4), (1, 8)))
    block_mask = set_ends((jax.random.randint(key_of[3], (D // BLOCK, FF // BLOCK), 0, 10) < 3).astype(jnp.int32), jax.random.fold_in(key_of[3], 1), 0, 1)
    return {"tokens": tokens, "out_grad": out_grad, "weight": weight, "block_mask": block_mask}


def reference(tokens, out_grad, weight, block_mask):
    keep_blocks = block_mask.astype(jnp.float32)
    width = FF // N_COL
    block_cols = width // BLOCK
    block_rows = D // BLOCK

    def one_group(accum, group_index):
        offset = (group_index * width).astype(jnp.int32)
        weight_panel = lax.dynamic_slice_in_dim(weight, offset, width, 1).astype(jnp.float32)
        keep_panel = lax.dynamic_slice_in_dim(keep_blocks, (group_index * block_cols).astype(jnp.int32), block_cols, 1)
        masked = (weight_panel.reshape(block_rows, BLOCK, block_cols, BLOCK) * keep_panel[:, None, :, None]).reshape(D, width).astype(jnp.bfloat16)
        grad_panel = lax.dynamic_slice_in_dim(out_grad, offset, width, 1)
        partial_value = lax.dot_general(grad_panel, masked, (((1,), (1,)), ((), ())), preferred_element_type=jnp.float32)
        accum = accum + partial_value.astype(jnp.bfloat16).astype(jnp.float32)
        full_grad = lax.dot_general(tokens, grad_panel, (((0,), (0,)), ((), ())), preferred_element_type=jnp.float32)
        kept_grad = (full_grad.reshape(block_rows, BLOCK, block_cols, BLOCK) * keep_panel[:, None, :, None]).reshape(D, width)
        return accum, kept_grad.astype(jnp.bfloat16)

    start_sum = jnp.zeros((tokens.shape[0], D), jnp.float32)
    accum, grads = lax.scan(one_group, start_sum, jnp.arange(N_COL, dtype=jnp.int32))
    weight_grad = jnp.transpose(grads, (1, 0, 2)).reshape(D, FF)
    return accum.astype(jnp.bfloat16), weight_grad
```

```python
import functools

import jax
import jax.numpy as jnp
from jax import lax
from jax.experimental import pallas as pl
from jax.experimental.pallas import tpu as pltpu
from jax.sharding import PartitionSpec as P

BLOCK = 256
SLOTS = 32
OUT_SLOTS = 16
UNROLL = 4
VMEM_LIMIT = 50 * 1024 * 1024
ANY = pl.BlockSpec(memory_space=pl.ANY)
SMEM = pl.BlockSpec(memory_space=pltpu.SMEM)
VMEM = pl.BlockSpec(memory_space=pltpu.VMEM)


def params():
    return pltpu.CompilerParams(vmem_limit_bytes=VMEM_LIMIT)


def span(index, size):
    return pl.ds(pl.multiple_of(index * size, size), size)


def columns_of(index):
    return span(index, BLOCK)


def prepare_kernel(mask, kept, starts, grad, zeros, sem):
    rows, cols = mask.shape
    zeros[...] = jnp.zeros_like(zeros)
    copies = [pltpu.make_async_copy(zeros, grad.at[pl.ds(i * BLOCK, BLOCK)], sem.at[i]) for i in range(rows)]
    for copy in copies:
        copy.start()

    def of_column(j, count):
        starts[j] = count

        def of_row(i, count):
            kept[count] = i * cols + j
            return count + jnp.where(mask[i, j] != 0, 1, 0)

        return lax.fori_loop(0, rows, of_row, count)

    starts[cols] = lax.fori_loop(0, cols, of_column, 0)
    for copy in copies:
        copy.wait()


def prepare(mask):
    rows, cols = mask.shape
    return pl.pallas_call(
        prepare_kernel,
        out_shape=(
            jax.ShapeDtypeStruct((rows * cols,), jnp.int32),
            jax.ShapeDtypeStruct((cols + 1,), jnp.int32),
            jax.ShapeDtypeStruct((rows * BLOCK, cols * BLOCK), jnp.bfloat16),
        ),
        in_specs=[SMEM],
        out_specs=(SMEM, SMEM, ANY),
        scratch_shapes=[pltpu.VMEM((BLOCK, cols * BLOCK), jnp.bfloat16), pltpu.SemaphoreType.DMA((rows,))],
        compiler_params=params(),
        name="prepare",
    )(mask)


def input_kernel(first, last, cols, peers, has_total, has_pieces, place, kept, starts, grads, weight, *rest):
    rest = list(rest)
    total_in = rest.pop(0) if has_total else None
    outs = [rest.pop(0) for _ in range(peers if has_pieces else 1)]
    held, blocks, total, grad_sem, block_sem, total_sem = rest
    part = last - first
    grad_copies = [
        pltpu.make_async_copy(grads.at[:, pl.ds(j * BLOCK, BLOCK)], held.at[j], grad_sem.at[j]) for j in range(part)
    ]
    start, end = starts[first], starts[last]
    count = end - start

    def block_copy(k):
        code = kept[start + k]
        i, j = code // cols, code % cols
        slot = lax.rem(k, SLOTS)
        return pltpu.make_async_copy(
            weight.at[columns_of(i), columns_of(j)], blocks.at[slot], block_sem.at[slot]
        )

    for copy in grad_copies:
        copy.start()

    @pl.loop(0, jnp.minimum(count, SLOTS))
    def _(k):
        block_copy(k).start()

    if has_total:
        pltpu.make_async_copy(total_in, total, total_sem).start()
        pltpu.make_async_copy(total_in, total, total_sem).wait()
    else:
        total[...] = jnp.zeros_like(total)
    for copy in grad_copies:
        copy.wait()

    @pl.loop(0, (count + UNROLL - 1) // UNROLL)
    def _(step):
        rows, sums = [], []
        for u in range(UNROLL):
            k = step * UNROLL + u

            @pl.when(k < count)
            def _():
                block_copy(k).wait()

        for u in range(UNROLL):
            k = step * UNROLL + u
            code = kept[start + jnp.minimum(k, count - 1)]
            i, j = code // cols, code % cols
            product = lax.dot_general(
                held[j - first],
                blocks[lax.rem(k, SLOTS)],
                (((1,), (1,)), ((), ())),
                preferred_element_type=jnp.float32,
            )
            rows.append(i)
            sums.append(jnp.where(k < count, product, 0.0))
        for i, product in zip(rows, sums):
            total[i] += product
        for u in range(UNROLL):
            k = step * UNROLL + u + SLOTS

            @pl.when(k < count)
            def _():
                block_copy(k).start()

    if not has_pieces:
        copy = pltpu.make_async_copy(total, outs[0], total_sem)
        copy.start()
        copy.wait()
        return
    me = place[0]
    size = outs[0].shape[0]
    for d, out in enumerate(outs):
        for i in range(total.shape[0]):
            out[:, pl.ds(i * BLOCK, BLOCK)] = total[i, span(me ^ d, size), :].astype(out.dtype)


def input_part(place, kept, starts, grads, weight, total, first, last, peers, has_pieces):
    tokens = grads.shape[0]
    rows, cols = weight.shape[0] // BLOCK, weight.shape[1] // BLOCK
    part = last - first
    if has_pieces:
        out_shape = [jax.ShapeDtypeStruct((tokens // peers, rows * BLOCK), jnp.bfloat16)] * peers
        out_specs = [VMEM] * peers
    else:
        out_shape = [jax.ShapeDtypeStruct((rows, tokens, BLOCK), jnp.float32)]
        out_specs = [ANY]
    has_total = total is not None
    return pl.pallas_call(
        functools.partial(input_kernel, first, last, cols, peers, has_total, has_pieces),
        out_shape=out_shape,
        in_specs=[SMEM, SMEM, SMEM, ANY, ANY] + [ANY] * has_total,
        out_specs=out_specs,
        scratch_shapes=[
            pltpu.VMEM((part, tokens, BLOCK), jnp.bfloat16),
            pltpu.VMEM((SLOTS, BLOCK, BLOCK), jnp.bfloat16),
            pltpu.VMEM((rows, tokens, BLOCK), jnp.float32),
            pltpu.SemaphoreType.DMA((part,)),
            pltpu.SemaphoreType.DMA((SLOTS,)),
            pltpu.SemaphoreType.DMA,
        ],
        compiler_params=params(),
        cost_estimate=pl.CostEstimate(
            flops=2 * tokens * rows * part * BLOCK * BLOCK,
            bytes_accessed=2 * rows * part * BLOCK * BLOCK,
            transcendentals=0,
        ),
        name="input_part",
    )(place, kept, starts, grads, weight, *([total] if has_total else []))


def weight_kernel(first, last, cols, offsets, kept, starts, tokens, *rest):
    grads = rest[: len(offsets)]
    _, grad, held, blocks, held_sem, out_sem = rest[len(offsets) :]
    part = last - first
    copies = []
    for j in range(part):
        spot = 0
        for source, offset in zip(grads, offsets):
            size = source.shape[0]
            copies.append(
                pltpu.make_async_copy(
                    source.at[:, pl.ds(offset + j * BLOCK, BLOCK)], held.at[j, pl.ds(spot, size)], held_sem.at[len(copies)]
                )
            )
            spot += size
    for copy in copies:
        copy.start()
    start, end = starts[first], starts[last]
    count = end - start

    def out_copy(k):
        code = kept[start + k]
        i, j = code // cols, code % cols
        slot = lax.rem(k, OUT_SLOTS)
        return pltpu.make_async_copy(blocks.at[slot], grad.at[columns_of(i), columns_of(j)], out_sem.at[slot])

    for copy in copies:
        copy.wait()

    @pl.loop(0, (count + UNROLL - 1) // UNROLL)
    def _(step):
        for u in range(UNROLL):
            k = step * UNROLL + u

            @pl.when((k >= OUT_SLOTS) & (k - OUT_SLOTS < count))
            def _():
                out_copy(k - OUT_SLOTS).wait()

        for u in range(UNROLL):
            k = step * UNROLL + u
            code = kept[start + jnp.minimum(k, count - 1)]
            i, j = code // cols, code % cols
            product = jnp.dot(tokens[i], held[j - first], preferred_element_type=jnp.float32)
            blocks[lax.rem(k, OUT_SLOTS)] = product.astype(blocks.dtype)
        for u in range(UNROLL):
            k = step * UNROLL + u

            @pl.when(k < count)
            def _():
                out_copy(k).start()

    done = (count + UNROLL - 1) // UNROLL * UNROLL

    @pl.loop(jnp.maximum(done - OUT_SLOTS, 0), count)
    def _(k):
        out_copy(k).wait()


def weight_part(kept, starts, tokens, grads, offsets, grad, first, last):
    rows, cols = grad.shape[0] // BLOCK, grad.shape[1] // BLOCK
    count = tokens.shape[2]
    part = last - first
    return pl.pallas_call(
        functools.partial(weight_kernel, first, last, cols, offsets),
        out_shape=jax.ShapeDtypeStruct(grad.shape, grad.dtype),
        in_specs=[SMEM, SMEM, VMEM] + [ANY] * len(grads) + [ANY],
        out_specs=ANY,
        scratch_shapes=[
            pltpu.VMEM((part, count, BLOCK), jnp.bfloat16),
            pltpu.VMEM((OUT_SLOTS, BLOCK, BLOCK), jnp.bfloat16),
            pltpu.SemaphoreType.DMA((part * len(grads),)),
            pltpu.SemaphoreType.DMA((OUT_SLOTS,)),
        ],
        input_output_aliases={3 + len(grads): 0},
        compiler_params=params(),
        cost_estimate=pl.CostEstimate(
            flops=2 * count * rows * part * BLOCK * BLOCK,
            bytes_accessed=2 * rows * part * BLOCK * BLOCK,
            transcendentals=0,
        ),
        name="weight_part",
    )(kept, starts, tokens, *grads, grad)


def assemble_kernel(sizes, place, *refs):
    *pieces, out = refs
    me = place[0]
    peers = len(pieces)
    for d, piece in enumerate(pieces):
        begin, spot = 0, 0
        for size in sizes:
            out[pl.ds(pl.multiple_of(spot + (me ^ d) * size, size), size), :] = piece[begin : begin + size, :]
            begin += size
            spot += size * peers


def assemble(place, pieces, sizes):
    peers, (size, width) = len(pieces), pieces[0].shape
    return pl.pallas_call(
        functools.partial(assemble_kernel, sizes),
        out_shape=jax.ShapeDtypeStruct((peers * size, width), pieces[0].dtype),
        in_specs=[SMEM] + [VMEM] * peers,
        out_specs=VMEM,
        compiler_params=params(),
        name="assemble",
    )(place, *pieces)


def exchange(pieces):
    peers = len(pieces)
    return [pieces[0]] + [
        lax.ppermute(pieces[d], "col", [(c, c ^ d) for c in range(peers)]) for d in range(1, peers)
    ]


def local(peers, tokens, out_grad, weight, block_mask):
    share, width = tokens.shape
    hidden = out_grad.shape[1]
    cols = hidden // BLOCK
    sizes = (share // 2, share // 4, share // 4)
    parts = ((0, cols // 2), (cols // 2, cols))
    place = lax.axis_index("col").astype(jnp.int32).reshape(1)

    shaped = out_grad.reshape(-1, share, hidden)
    gathered, begin = [], 0
    for n, size in enumerate(sizes):
        group = shaped[:, begin : begin + size].reshape(-1, hidden)
        begin += size
        if n < len(sizes) - 1:
            gathered.append(lax.all_gather(group, "row", axis=0, tiled=True))
        else:
            finals = [
                lax.all_gather(group[:, a * BLOCK : b * BLOCK], "row", axis=0, tiled=True) for a, b in parts
            ]

    features = assemble(place, exchange([tokens] * peers), sizes)
    features = features.T.reshape(width // BLOCK, BLOCK, -1)
    kept, starts, weight_grad = prepare(block_mask)

    sums = []
    for grads in gathered:
        pieces = input_part(place, kept, starts, grads, weight, None, 0, cols, peers, True)
        sums.append(exchange(pieces))

    total = None
    for n, (a, b) in enumerate(parts):
        ending = n == len(parts) - 1
        result = input_part(place, kept, starts, finals[n], weight, total, a, b, peers, ending)
        if ending:
            sums.append(exchange(result))
        else:
            total = result[0]
        weight_grad = weight_part(
            kept, starts, features, gathered + [finals[n]], [a * BLOCK] * len(gathered) + [0], weight_grad, a, b
        )
    input_grad = jnp.concatenate(
        [sum(piece.astype(jnp.float32) for piece in pieces).astype(jnp.bfloat16) for pieces in sums], axis=0
    )
    return input_grad, weight_grad


def solution(mesh):
    in_specs = (P("col", "row"), P("row", "col"), P("row", "col"), P("row", "col"))
    out_specs = (P("col", "row"), P("row", "col"))
    return jax.shard_map(
        functools.partial(local, mesh.shape["col"]), mesh=mesh, in_specs=in_specs, out_specs=out_specs, check_vma=False
    )
```
